32 devices in a mesh: seq: 16 (over z, x, core), tp: 2 (over y).
Axes of the slice: x: 2, y: 2, z: 4, core: 2. Of those that a mesh axis runs over, the one named last changes fastest.
Arguments:
- acts: bfloat16 [8192, 4608], P('seq', 'tp'), may hold values from -6 to 6
- attn: bfloat16 [8192, 4096], P('seq', 'tp'), may hold values from -6 to 6
- teacher: bfloat16 [8192, 3584], P('seq', 'tp'), may hold values from -6 to 6
- out_weight: bfloat16 [4096, 4608], P('tp'), may hold values from -0.09375 to 0.09375
- proj_weight: bfloat16 [3584, 4608], P('tp'), may hold values from -0.09375 to 0.09375
Outputs:
- attn_grad: bfloat16 [8192, 4096], P('seq', 'tp')
- out_grad: bfloat16 [4096, 4608], P('tp', 'seq')
- proj_grad: bfloat16 [3584, 4608], P('tp', 'seq')
The draws below stay inside these ranges and needn't reach their ends.
All inputs are finite; a program needn't handle non-finite values.
Results may differ from the reference program's by a relative error of at most 0.015.
Values may be sent and summed in bfloat16 or wider, within the bound.
A program may use at most 192 MiB of HBM per device.

```python
import jax
import jax.numpy as jnp
from jax import lax

DS = 4608
ATT = 4096
DT = 3584
TOK_DEV = 512
TOKENS = 8192
N_SEQ = 16
N_TP = 2


def block_scale(own_key, dims, split, least, largest):
    factor_of = 1.0
    for position, parts in split:
        steps = jax.random.uniform(jax.random.fold_in(jax.random.fold_in(own_key, 6), position), (parts,), jnp.float32, least / len(split), largest / len(split))
        factor_of = factor_of * jnp.repeat(jnp.exp(steps), dims[position] // parts).reshape((-1,) + (1,) * (len(dims) - 1 - position))
    return factor_of


def centred(key, dims, spread, reach, split=(), kind=jnp.bfloat16):
    level = block_scale(key, dims, split, -0.22, 0.18) if split else 1.0
    result = jax.random.normal(key, dims, jnp.float32) * spread * level
    return jnp.minimum(jnp.maximum(result, -reach), reach).astype(kind)


def setup_inputs(seed: int = 0) -> dict:
    key_list = jax.random.split(jax.random.key(seed), 6)
    acts = centred(key_list[0], (TOKENS, DS), 1.0, 6.0, ((0, 16), (1, 2)))
    attn = centred(key_list[1], (TOKENS, ATT), 1.0, 6.0, ((0, 16), (1, 2)))
    teacher = centred(key_list[2], (TOKENS, DT), 1.0, 6.0, ((0, 16), (1, 2)))
    out_weight = centred(key_list[3], (ATT, DS), ATT ** -0.5, 0.09375, ((0, 2),))
    proj_weight = centred(key_list[4], (DT, DS), DT ** -0.5, 0.09375, ((0, 2),))
    return dict(acts=acts, attn=attn, teacher=teacher, out_weight=out_weight, proj_weight=proj_weight)


def reference(acts, attn, teacher, out_weight, proj_weight):
    att_block = ATT // N_TP
    dt_block = DT // N_TP
    total = acts.astype(jnp.float32)
    for j in range(N_TP):
        student = jnp.dot(attn[:, j * att_block:(j + 1) * att_block], out_weight[j * att_block:(j + 1) * att_block], preferred_element_type=jnp.float32)
        mapped = jnp.dot(teacher[:, j * dt_block:(j + 1) * dt_block], proj_weight[j * dt_block:(j + 1) * dt_block], preferred_element_type=jnp.float32)
        rounded = lax.optimization_barrier((student - mapped).astype(jnp.bfloat16))
        total = total + rounded.astype(jnp.float32)
    resid_grad = total.astype(jnp.bfloat16)
    attn_grad = lax.dot_general(resid_grad, out_weight, (((1,), (1,)), ((), ())), preferred_element_type=jnp.float32).astype(jnp.bfloat16)

    def accumulate(carry, index):
        start = (index * TOK_DEV).astype(jnp.int32)
        attn_rows = lax.dynamic_slice_in_dim(attn, start, TOK_DEV, 0)
        teacher_rows = lax.dynamic_slice_in_dim(teacher, start, TOK_DEV, 0)
        grad_rows = lax.dynamic_slice_in_dim(resid_grad, start, TOK_DEV, 0)
        out_term = lax.dot_general(attn_rows, grad_rows, (((0,), (0,)), ((), ())), preferred_element_type=jnp.float32)
        proj_term = -lax.dot_general(teacher_rows, grad_rows, (((0,), (0,)), ((), ())), preferred_element_type=jnp.float32)
        out_term = lax.optimization_barrier(out_term.astype(jnp.bfloat16)).astype(jnp.float32)
        proj_term = lax.optimization_barrier(proj_term.astype(jnp.bfloat16)).astype(jnp.float32)
        return (carry[0] + out_term, carry[1] + proj_term), None

    start_sums = (jnp.zeros((ATT, DS), jnp.float32), jnp.zeros((DT, DS), jnp.float32))
    sums, unused = lax.scan(accumulate, start_sums, jnp.arange(N_SEQ, dtype=jnp.int32))
    return attn_grad, sums[0].astype(jnp.bfloat16), sums[1].astype(jnp.bfloat16)
```

```python
import functools

import jax
import jax.numpy as jnp
from jax import lax
from jax.sharding import PartitionSpec as P

F32 = jnp.float32
BF16 = jnp.bfloat16


def generic(acts, attn, teacher, out_weight, proj_weight):
    joined = jnp.dot(attn, out_weight, preferred_element_type=F32) - jnp.dot(
        teacher, proj_weight, preferred_element_type=F32
    )
    totals = lax.psum(joined.astype(BF16), "tp").astype(F32)
    whole_acts = lax.all_gather(acts, "tp", axis=1, tiled=True)
    resid_grad = (whole_acts.astype(F32) + totals).astype(BF16)
    attn_grad = lax.dot_general(
        resid_grad, out_weight, (((1,), (1,)), ((), ())), preferred_element_type=F32
    ).astype(BF16)
    out_terms = lax.dot_general(
        attn, resid_grad, (((0,), (0,)), ((), ())), preferred_element_type=F32
    )
    proj_terms = -lax.dot_general(
        teacher, resid_grad, (((0,), (0,)), ((), ())), preferred_element_type=F32
    )
    return (
        attn_grad,
        lax.psum_scatter(out_terms.astype(BF16), "seq", scatter_dimension=1, tiled=True),
        lax.psum_scatter(proj_terms.astype(BF16), "seq", scatter_dimension=1, tiled=True),
    )


def add(a, b):
    return (a.astype(F32) + b.astype(F32)).astype(BF16)


def local(acts, attn, teacher, out_weight, proj_weight):
    s = lax.axis_index("seq")
    tp = lax.axis_index("tp")
    core, x, z = s % 2, (s // 2) % 2, s // 4
    ds = out_weight.shape[1]
    width = ds // 4
    strip = width // 4
    half = acts.shape[1]
    features = attn.shape[1]
    both = jnp.concatenate([attn, -teacher], axis=1)
    core_pairs = [(i, i ^ 1) for i in range(16)]
    x_pairs = [(i, i ^ 2) for i in range(16)]
    hops = {
        0: [[(3, 2)], [(2, 1)], [(1, 0)]],
        1: [[(3, 2), (0, 1)], [(2, 1)]],
        2: [[(0, 1), (3, 2)], [(1, 2)]],
        3: [[(0, 1)], [(1, 2)], [(2, 3)]],
    }
    order = [0, 3, 1, 2]
    resid = {}
    for k in order:
        cols = slice(k * width, (k + 1) * width)
        part = jnp.dot(attn, out_weight[:, cols], preferred_element_type=F32) - jnp.dot(
            teacher, proj_weight[:, cols], preferred_element_type=F32
        )
        own, at = divmod(k * width, half)
        mine = jnp.where(tp == own, acts[:, at : at + width].astype(F32), 0.0)
        part = (part + mine).astype(BF16)
        other = lax.ppermute(part, "tp", [(0, 1), (1, 0)])
        resid[k] = add(part, other)
    total = None
    for k in order:
        terms = lax.dot_general(
            resid[k], both, (((0,), (0,)), ((), ())), preferred_element_type=F32
        ).astype(BF16)
        terms = terms.reshape(2, 2, strip, -1)
        keep = lax.dynamic_index_in_dim(terms, core, 1, keepdims=False)
        send = lax.dynamic_index_in_dim(terms, 1 - core, 1, keepdims=False)
        chip = add(keep, lax.ppermute(send, "seq", core_pairs))
        keep = lax.dynamic_index_in_dim(chip, x, 0, keepdims=False)
        send = lax.dynamic_index_in_dim(chip, 1 - x, 0, keepdims=False)
        line = add(keep, lax.ppermute(send, "seq", x_pairs))
        for hop in hops[k]:
            pairs = [(a * 4 + i, b * 4 + i) for a, b in hop for i in range(4)]
            line = add(line, lax.ppermute(line, "seq", pairs))
        total = line if total is None else jnp.where(z == k, line, total)
    whole = jnp.concatenate([resid[k] for k in range(4)], axis=1)
    attn_grad = lax.dot_general(
        whole, out_weight, (((1,), (1,)), ((), ())), preferred_element_type=F32
    ).astype(BF16)
    total = total.T
    return attn_grad, total[:features], total[features:]


def solution(mesh):
    placed = (P("seq", "tp"), P("seq", "tp"), P("seq", "tp"), P("tp", None), P("tp", None))
    tuned = mesh.shape["seq"] == 16 and mesh.shape["tp"] == 2
    return jax.shard_map(
        local if tuned else generic,
        mesh=mesh,
        in_specs=placed,
        out_specs=(P("seq", "tp"), P("tp", "seq"), P("tp", "seq")),
        check_vma=False,
    )
```

```python
import functools

import jax
import jax.numpy as jnp
from jax import lax
from jax.sharding import PartitionSpec as P

F32 = jnp.float32
BF16 = jnp.bfloat16


def generic(acts, attn, teacher, out_weight, proj_weight):
    joined = jnp.dot(attn, out_weight, preferred_element_type=F32) - jnp.dot(
        teacher, proj_weight, preferred_element_type=F32
    )
    totals = lax.psum(joined.astype(BF16), "tp").astype(F32)
    whole_acts = lax.all_gather(acts, "tp", axis=1, tiled=True)
    resid_grad = (whole_acts.astype(F32) + totals).astype(BF16)
    attn_grad = lax.dot_general(
        resid_grad, out_weight, (((1,), (1,)), ((), ())), preferred_element_type=F32
    ).astype(BF16)
    out_terms = lax.dot_general(
        attn, resid_grad, (((0,), (0,)), ((), ())), preferred_element_type=F32
    )
    proj_terms = -lax.dot_general(
        teacher, resid_grad, (((0,), (0,)), ((), ())), preferred_element_type=F32
    )
    return (
        attn_grad,
        lax.psum_scatter(out_terms.astype(BF16), "seq", scatter_dimension=1, tiled=True),
        lax.psum_scatter(proj_terms.astype(BF16), "seq", scatter_dimension=1, tiled=True),
    )


def add(a, b):
    return (a.astype(F32) + b.astype(F32)).astype(BF16)


def after(value, *needs):
    return lax.optimization_barrier((value,) + needs)[0]


def local(acts, attn, teacher, out_weight, proj_weight):
    s = lax.axis_index("seq")
    tp = lax.axis_index("tp")
    core, x, z = s % 2, (s // 2) % 2, s // 4
    width = out_weight.shape[1] // 4
    strip = width // 4
    half = acts.shape[1]
    core_pairs = [(i, i ^ 1) for i in range(16)]
    x_pairs = [(i, i ^ 2) for i in range(16)]
    hops = {
        0: [[(3, 2)], [(2, 1)], [(1, 0)]],
        1: [[(3, 2), (0, 1)], [(2, 1)]],
        2: [[(0, 1), (3, 2)], [(1, 2)]],
        3: [[(0, 1)], [(1, 2)], [(2, 3)]],
    }
    order = [0, 3, 1, 2]

    def partial(k, *needs):
        cols = slice(k * width, (k + 1) * width)
        a, t = (after(attn, *needs), after(teacher, *needs)) if needs else (attn, teacher)
        part = jnp.dot(a, out_weight[:, cols], preferred_element_type=F32) - jnp.dot(
            t, proj_weight[:, cols], preferred_element_type=F32
        )
        own, at = divmod(k * width, half)
        mine = jnp.where(tp == own, acts[:, at : at + width].astype(F32), 0.0)
        return (part + mine).astype(BF16)

    def over_tp(part):
        return add(part, lax.ppermute(part, "tp", [(0, 1), (1, 0)]))

    def terms(grad, features, sign):
        value = sign * lax.dot_general(
            grad, features, (((0,), (0,)), ((), ())), preferred_element_type=F32
        )
        value = value.astype(BF16).reshape(2, 2, strip, -1)
        keep = lax.dynamic_index_in_dim(value, core, 1, keepdims=False)
        send = lax.dynamic_index_in_dim(value, 1 - core, 1, keepdims=False)
        return keep, send

    resid, chip, line = {}, {}, {}
    hop_done = {}
    parts = {0: partial(order[0]), 1: None}
    parts[1] = partial(order[1])
    resid[0] = over_tp(parts[0])
    pieces = []
    attn_grad = None

    def advance(n, stage):
        if n < 0:
            return None
        steps = hops[order[n // 2]]
        if stage >= len(steps):
            return None
        pairs = [(a * 4 + i, b * 4 + i) for a, b in steps[stage] for i in range(4)]
        line[n] = add(line[n], lax.ppermute(line[n], "seq", pairs))
        return line[n]

    for i in range(4):
        keep_send = [terms(resid[i], attn, 1.0), terms(resid[i], teacher, -1.0)]
        if i + 1 < 4:
            resid[i + 1] = over_tp(after(parts[i + 1], resid[i]))
        if i + 2 < 4:
            parts[i + 2] = partial(order[i + 2], keep_send[0][1], keep_send[1][1])
        for j in range(2):
            n = 2 * i + j
            keep, send = keep_send[j]
            chip[n] = add(keep, lax.ppermute(send, "seq", core_pairs))
        if i == 3:
            whole = jnp.concatenate([resid[order.index(k)] for k in range(4)], axis=1)
            attn_grad = lax.dot_general(
                whole, out_weight, (((1,), (1,)), ((), ())), preferred_element_type=F32
            ).astype(BF16)
        for j in range(2):
            n = 2 * i + j
            needs = [line[n - 2]] if n >= 2 else []
            for back, stage in ((4, 0), (5, 1), (6, 2)):
                moved = advance(n - back, stage)
                if moved is not None:
                    needs.append(moved)
            if n == 7:
                needs.append(attn_grad)
            value = after(chip[n], *needs) if needs else chip[n]
            keep = lax.dynamic_index_in_dim(value, x, 0, keepdims=False)
            send = lax.dynamic_index_in_dim(value, 1 - x, 0, keepdims=False)
            line[n] = add(keep, lax.ppermute(send, "seq", x_pairs))
    for n in range(8, 14):
        for back, stage in ((4, 0), (5, 1), (6, 2)):
            if n - back < 8:
                advance(n - back, stage)
    grads = []
    for j in range(2):
        total = line[j]
        for i in range(1, 4):
            total = jnp.where(z == order[i], line[2 * i + j], total)
        grads.append(total.T)
    return attn_grad, grads[0], grads[1]


def solution(mesh):
    placed = (P("seq", "tp"), P("seq", "tp"), P("seq", "tp"), P("tp", None), P("tp", None))
    tuned = mesh.shape["seq"] == 16 and mesh.shape["tp"] == 2
    return jax.shard_map(
        local if tuned else generic,
        mesh=mesh,
        in_specs=placed,
        out_specs=(P("seq", "tp"), P("tp", "seq"), P("tp", "seq")),
        check_vma=False,
    )
```

```python
import functools

import jax
import jax.numpy as jnp
from jax import lax
from jax.sharding import PartitionSpec as P

F32 = jnp.float32
BF16 = jnp.bfloat16


def generic(acts, attn, teacher, out_weight, proj_weight):
    joined = jnp.dot(attn, out_weight, preferred_element_type=F32) - jnp.dot(
        teacher, proj_weight, preferred_element_type=F32
    )
    totals = lax.psum(joined.astype(BF16), "tp").astype(F32)
    whole_acts = lax.all_gather(acts, "tp", axis=1, tiled=True)
    resid_grad = (whole_acts.astype(F32) + totals).astype(BF16)
    attn_grad = lax.dot_general(
        resid_grad, out_weight, (((1,), (1,)), ((), ())), preferred_element_type=F32
    ).astype(BF16)
    out_terms = lax.dot_general(
        attn, resid_grad, (((0,), (0,)), ((), ())), preferred_element_type=F32
    )
    proj_terms = -lax.dot_general(
        teacher, resid_grad, (((0,), (0,)), ((), ())), preferred_element_type=F32
    )
    return (
        attn_grad,
        lax.psum_scatter(out_terms.astype(BF16), "seq", scatter_dimension=1, tiled=True),
        lax.psum_scatter(proj_terms.astype(BF16), "seq", scatter_dimension=1, tiled=True),
    )


def add(a, b):
    return (a.astype(F32) + b.astype(F32)).astype(BF16)


def after(value, *needs):
    return lax.optimization_barrier((value,) + needs)[0]


def local(acts, attn, teacher, out_weight, proj_weight):
    s = lax.axis_index("seq")
    tp = lax.axis_index("tp")
    core, x, z = s % 2, (s // 2) % 2, s // 4
    z_low, z_high = z % 2, z // 2
    width = out_weight.shape[1] // 4
    strip = width // 4
    half = acts.shape[1]
    mid = attn.shape[1] // 2

    def swap(value, bit):
        return lax.ppermute(value, "seq", [(i, i ^ bit) for i in range(16)])

    def partial(k, *needs):
        cols = slice(k * width, (k + 1) * width)
        a, t = (after(attn, *needs), after(teacher, *needs)) if needs else (attn, teacher)
        part = jnp.dot(a, out_weight[:, cols], preferred_element_type=F32) - jnp.dot(
            t, proj_weight[:, cols], preferred_element_type=F32
        )
        own, at = divmod(k * width, half)
        mine = jnp.where(tp == own, acts[:, at : at + width].astype(F32), 0.0)
        return (part + mine).astype(BF16)

    def over_core(grad, features, sign):
        value = sign * lax.dot_general(
            grad, features, (((0,), (0,)), ((), ())), preferred_element_type=F32
        )
        value = value.astype(BF16).reshape(2, 2, strip, -1)
        keep = lax.dynamic_index_in_dim(value, core, 1, keepdims=False)
        send = lax.dynamic_index_in_dim(value, 1 - core, 1, keepdims=False)
        return keep, send, swap(send, 1)

    sent = {}
    line = {}

    def over_x(k, group, chip, *needs):
        keep = lax.dynamic_index_in_dim(chip, x, 0, keepdims=False)
        send = lax.dynamic_index_in_dim(chip, 1 - x, 0, keepdims=False)
        sent[k, group] = after(send, *needs) if needs else send
        line[k, group] = add(keep, swap(sent[k, group], 2))

    pair_sent = {}

    def over_z_low(low, group):
        even, odd = line[low, group], line[low + 1, group]
        send = jnp.where(z_low == 0, odd, even)
        pair_sent[low, group] = send
        return add(jnp.where(z_low == 0, even, odd), swap(send, 4))

    def over_z_high(first, second):
        send = jnp.where(z_high == 0, second, first)
        return add(jnp.where(z_high == 0, first, second), swap(send, 8))

    def over_tp(part):
        return lax.ppermute(part, "tp", [(0, 1), (1, 0)])

    parts = [partial(0), partial(1), None, None]
    other = [over_tp(parts[0]), None, None, None]
    resid, chip_t, chip_a = [], [], []
    for k in range(4):
        if k == 0:
            landed = after(other[0], parts[1])
        elif k == 1:
            landed = after(other[1], line[0, "t"], sent[0, "b"], parts[2])
        elif k == 2:
            landed = after(other[2], line[0, "b"], sent[1, "a"], parts[3])
        else:
            landed = after(other[3], line[1, "t"], sent[2, "t"])
        resid.append(add(parts[k], landed))
        if k < 3:
            other[k + 1] = over_tp(after(parts[k + 1], landed))
        keep_t, send_t, got_t = over_core(resid[k], teacher, -1.0)
        keep_a, send_a, got_a = over_core(resid[k], attn, 1.0)
        if k + 2 < 4:
            parts[k + 2] = partial(k + 2, send_t, send_a)
        chip_t.append(add(keep_t, got_t))
        chip_a.append(add(keep_a, got_a))
        if k == 1:
            over_x(1, "t", chip_t[1], line[0, "a"])
            over_x(1, "a", chip_a[1][..., :mid], line[0, "b"])
        else:
            over_x(k, "t", chip_t[k])
        if k == 0:
            over_x(0, "a", chip_a[0][..., :mid])
            over_x(0, "b", chip_a[0][..., mid:])
    pair = {(0, "t"): over_z_low(0, "t")}
    over_x(2, "a", chip_a[2][..., :mid], line[1, "a"])
    over_x(3, "a", chip_a[3][..., :mid], line[1, "a"])
    pair[0, "a"] = over_z_low(0, "a")
    over_x(1, "b", chip_a[1][..., mid:], line[2, "t"], pair_sent[0, "a"])
    over_x(2, "b", chip_a[2][..., mid:], line[3, "t"], pair[0, "t"])
    over_x(3, "b", chip_a[3][..., mid:], line[3, "t"], pair[0, "a"])
    pair[2, "t"] = over_z_low(2, "t")
    whole = after(jnp.concatenate(resid, axis=1), sent[3, "b"])
    attn_grad = lax.dot_general(
        whole, out_weight, (((1,), (1,)), ((), ())), preferred_element_type=F32
    ).astype(BF16)
    done = {}
    done["t"] = over_z_high(pair[0, "t"], pair[2, "t"])
    done["a"] = over_z_high(pair[0, "a"], over_z_low(2, "a"))
    done["b"] = over_z_high(over_z_low(0, "b"), over_z_low(2, "b"))
    out_grad = jnp.concatenate([done["a"].T, done["b"].T], axis=0)
    return attn_grad, out_grad, done["t"].T


def solution(mesh):
    placed = (P("seq", "tp"), P("seq", "tp"), P("seq", "tp"), P("tp", None), P("tp", None))
    tuned = mesh.shape["seq"] == 16 and mesh.shape["tp"] == 2
    return jax.shard_map(
        local if tuned else generic,
        mesh=mesh,
        in_specs=placed,
        out_specs=(P("seq", "tp"), P("tp", "seq"), P("tp", "seq")),
        check_vma=False,
    )
```

```python
import functools

import jax
import jax.numpy as jnp
from jax import lax
from jax.sharding import PartitionSpec as P

F32 = jnp.float32
BF16 = jnp.bfloat16


def generic(acts, attn, teacher, out_weight, proj_weight):
    joined = jnp.dot(attn, out_weight, preferred_element_type=F32) - jnp.dot(
        teacher, proj_weight, preferred_element_type=F32
    )
    totals = lax.psum(joined.astype(BF16), "tp").astype(F32)
    whole_acts = lax.all_gather(acts, "tp", axis=1, tiled=True)
    resid_grad = (whole_acts.astype(F32) + totals).astype(BF16)
    attn_grad = lax.dot_general(
        resid_grad, out_weight, (((1,), (1,)), ((), ())), preferred_element_type=F32
    ).astype(BF16)
    out_terms = lax.dot_general(
        attn, resid_grad, (((0,), (0,)), ((), ())), preferred_element_type=F32
    )
    proj_terms = -lax.dot_general(
        teacher, resid_grad, (((0,), (0,)), ((), ())), preferred_element_type=F32
    )
    return (
        attn_grad,
        lax.psum_scatter(out_terms.astype(BF16), "seq", scatter_dimension=1, tiled=True),
        lax.psum_scatter(proj_terms.astype(BF16), "seq", scatter_dimension=1, tiled=True),
    )


def add(a, b):
    return (a.astype(F32) + b.astype(F32)).astype(BF16)


def after(value, *needs):
    return lax.optimization_barrier((value,) + needs)[0]


def local(acts, attn, teacher, out_weight, proj_weight):
    s = lax.axis_index("seq")
    tp = lax.axis_index("tp")
    core, x, z = s % 2, (s // 2) % 2, s // 4
    z_low, z_high = z % 2, z // 2
    width = out_weight.shape[1] // 4
    strip = width // 4
    half = acts.shape[1]
    mid = attn.shape[1] // 2

    def swap(value, bit):
        return lax.ppermute(value, "seq", [(i, i ^ bit) for i in range(16)])

    def partial(k, *needs):
        cols = slice(k * width, (k + 1) * width)
        a, t = (after(attn, *needs), after(teacher, *needs)) if needs else (attn, teacher)
        part = jnp.dot(a, out_weight[:, cols], preferred_element_type=F32) - jnp.dot(
            t, proj_weight[:, cols], preferred_element_type=F32
        )
        own, at = divmod(k * width, half)
        mine = jnp.where(tp == own, acts[:, at : at + width].astype(F32), 0.0)
        return (part + mine).astype(BF16)

    def over_core(grad, features, sign, *needs):
        value = sign * lax.dot_general(
            grad, features, (((0,), (0,)), ((), ())), preferred_element_type=F32
        )
        value = value.astype(BF16).reshape(2, 2, strip, -1)
        keep = lax.dynamic_index_in_dim(value, core, 1, keepdims=False)
        send = lax.dynamic_index_in_dim(value, 1 - core, 1, keepdims=False)
        send = after(send, *needs) if needs else send
        return keep, send, swap(send, 1)

    sent = {}
    line = {}

    def over_x(k, groups, chips, *needs):
        chip = chips[0] if len(chips) == 1 else jnp.concatenate(chips, axis=-1)
        keep = lax.dynamic_index_in_dim(chip, x, 0, keepdims=False)
        send = lax.dynamic_index_in_dim(chip, 1 - x, 0, keepdims=False)
        send = after(send, *needs) if needs else send
        got = swap(send, 2)
        at = 0
        for group, piece in zip(groups, chips):
            cols = slice(at, at + piece.shape[-1])
            at += piece.shape[-1]
            sent[k, group] = send
            line[k, group] = add(keep[:, cols], got[:, cols])

    pair_sent = {}

    def over_z_low(low, group):
        even, odd = line[low, group], line[low + 1, group]
        send = jnp.where(z_low == 0, odd, even)
        pair_sent[low, group] = send
        return add(jnp.where(z_low == 0, even, odd), swap(send, 4))

    def over_z_high(first, second):
        send = jnp.where(z_high == 0, second, first)
        pair_sent["high"] = send
        return add(jnp.where(z_high == 0, first, second), swap(send, 8))

    def over_tp(part):
        return lax.ppermute(part, "tp", [(0, 1), (1, 0)])

    parts = [partial(0), partial(1), None, None]
    other = [over_tp(parts[0]), None, None, None]
    resid, chip_t, chip_a = [], [], []
    for k in range(4):
        if k == 0:
            landed = after(other[0], parts[1])
        elif k == 1:
            landed = after(other[1], line[0, "t"], sent[0, "b"], parts[2])
        elif k == 2:
            landed = after(other[2], line[0, "b"], sent[1, "t"], parts[3])
        else:
            landed = after(other[3], sent[2, "t"])
        resid.append(add(parts[k], landed))
        if k < 3:
            other[k + 1] = over_tp(after(parts[k + 1], other[k]))
        needs = {1: [line.get((0, "a"))], 3: [line.get((1, "t"))]}.get(k, [])
        keep_t, send_t, got_t = over_core(resid[k], teacher, -1.0, *needs)
        keep_a, send_a, got_a = over_core(resid[k], attn, 1.0, *needs)
        if k + 2 < 4:
            parts[k + 2] = partial(k + 2, send_t, send_a)
        chip_t.append(add(keep_t, got_t))
        chip_a.append(add(keep_a, got_a))
        low, high = chip_a[k][..., :mid], chip_a[k][..., mid:]
        if k == 0:
            over_x(0, "t", [chip_t[0]])
            over_x(0, "a", [low])
            over_x(0, "b", [high])
        elif k == 1:
            over_x(1, "ta", [chip_t[1], low], line[0, "b"])
        elif k == 2:
            over_x(2, "ta", [chip_t[2], low])
    over_x(3, "t", [chip_t[3]], sent[2, "t"], line[1, "t"])
    pair = {(0, "t"): over_z_low(0, "t"), (0, "a"): over_z_low(0, "a")}
    over_x(3, "a", [low], line[1, "t"], pair_sent[0, "t"], sent[3, "t"])
    over_x(1, "b", [chip_a[1][..., mid:]], line[1, "t"], sent[3, "a"])
    over_x(2, "b", [chip_a[2][..., mid:]], line[2, "t"], pair_sent[0, "a"], sent[3, "a"])
    pair[0, "b"] = over_z_low(0, "b")
    pair[2, "t"] = over_z_low(2, "t")
    over_x(3, "b", [high], line[3, "t"], pair[0, "t"], pair_sent[2, "t"])
    done = {"t": over_z_high(pair[0, "t"], pair[2, "t"])}
    whole = after(jnp.concatenate(resid, axis=1), sent[3, "b"], pair_sent["high"])
    attn_grad = lax.dot_general(
        whole, out_weight, (((1,), (1,)), ((), ())), preferred_element_type=F32
    ).astype(BF16)
    for group in ("a", "b"):
        done[group] = over_z_high(pair[0, group], over_z_low(2, group))
    out_grad = jnp.concatenate([done["a"].T, done["b"].T], axis=0)
    return attn_grad, out_grad, done["t"].T


def solution(mesh):
    placed = (P("seq", "tp"), P("seq", "tp"), P("seq", "tp"), P("tp", None), P("tp", None))
    tuned = mesh.shape["seq"] == 16 and mesh.shape["tp"] == 2
    return jax.shard_map(
        local if tuned else generic,
        mesh=mesh,
        in_specs=placed,
        out_specs=(P("seq", "tp"), P("tp", "seq"), P("tp", "seq")),
        check_vma=False,
    )
```
